32 devices in a mesh: dev: 32 (over z, y, x, core).
Axes of the slice: x: 2, y: 2, z: 4, core: 2. Of those that a mesh axis runs over, the one named last changes fastest.
Arguments:
- residual: float32 [32, 6, 32, 3072], P('dev'), may hold values from -60 to 60
- direction: float32 [32, 6, 32, 3072], P('dev'), may hold values from -60 to 60
- legendre_scalar: bfloat16 [32, 3072, 128], P('dev'), may hold values from -0.109375 to 0.109375
- legendre_plus: bfloat16 [32, 3072, 128], P('dev'), may hold values from -0.109375 to 0.109375
- legendre_minus: bfloat16 [32, 3072, 128], P('dev'), may hold values from -0.109375 to 0.109375
- prior_inverse: float32 [4, 3072], replicated, as said below
- noise_weight: float32 [128, 2, 3, 4096], P('dev'), may hold values from 0.00025 to 0.0025
- order_ids: int32 [32], replicated, may hold values from 1 to 1535, as said below
- live_blocks: int32 [32, 2], P('dev'), may hold values from 1 to 4
- cycle_assign: int32 [128], replicated, may hold values from 0 to 127, each once
- cycle_length: int32 [128], P('dev'), may hold values from 1024 to 4096, as said below
- cycle_shift: int32 [128], P('dev'), may hold values from 0 to 1
Outputs:
- residual_next: float32 [32, 6, 32, 3072], P('dev')
- direction_next: float32 [32, 6, 32, 3072], P('dev')
- step_length: float32 [32], replicated
The draws below stay inside these ranges and needn't reach their ends.
Inputs may be any that keep to these rules, and one draw needn't show every extreme that they name: `order_ids`: the values are distinct; each pair holds two different orders below 3072. `cycle_length`: multiples of 4. `cycle_assign`: each latitude pair appears once. `prior_inverse`: for every degree tt and ee are positive, bb is positive and te squared is below tt ee.
All inputs are finite; a program needn't handle non-finite values.
Results may differ from the reference program's by a relative error of at most 0.003.
Values may be sent and summed in bfloat16 or wider, within the bound.
A program may use at most 128 MiB of HBM per device.

```python
import math
import jax
import jax.numpy as jnp
from jax import lax

L = 3072
PIX = 4096
BLOCKS = 4
SIMS = 32
ORD_PAIRS = 32
ORDERS = 64
PAIRS = 128


def coefficient_scales(key):
    rows = jnp.arange(ORD_PAIRS, dtype=jnp.float32) / max(ORD_PAIRS - 1, 1)
    rise = 3.0 ** rows
    degree_scale = jnp.exp(jax.random.uniform(key, (ORD_PAIRS, 1, 1, L), minval=-1.15, maxval=1.15))
    return rise[:, None, None, None] * degree_scale


def draw_residual(key, part):
    key = jax.random.fold_in(key, 21)
    first, second = jax.random.split(key)
    base = jax.random.truncated_normal(first, -6.0, 6.0, (ORD_PAIRS, 6, SIMS, L))
    return base * coefficient_scales(second)


def draw_direction(key, part):
    key = jax.random.fold_in(key, 22)
    first, second = jax.random.split(key)
    base = jax.random.truncated_normal(first, -6.0, 6.0, (ORD_PAIRS, 6, SIMS, L))
    return base * coefficient_scales(second)


def draw_prior_inverse(key, part):
    key = jax.random.fold_in(key, 23)
    keys = jax.random.split(key, 2)
    autos = jnp.exp(jax.random.uniform(keys[0], (3, L), minval=-1.2, maxval=1.1))
    tie = jax.random.uniform(keys[1], (L,), minval=-0.6, maxval=0.6)
    cross = tie * jnp.sqrt(autos[0] * autos[1])
    return jnp.stack([autos[0], cross, autos[1], autos[2]])


def draw_order_ids(key, part):
    key = jax.random.fold_in(key, 24)
    first, second = jax.random.split(key)
    pool = jax.random.permutation(first, L // 2 - 3).astype(jnp.int32) + 2
    ends = jnp.array([1, L // 2 - 1], dtype=jnp.int32)
    chosen = jnp.concatenate([ends, pool[:ORD_PAIRS - 2]])
    return jax.random.permutation(second, chosen).astype(jnp.int32)


def draw_cycle_length(key, part):
    key = jax.random.fold_in(key, 25)
    keys = jax.random.split(key, 3)
    lengths = 4 * jax.random.randint(keys[0], (PAIRS,), PIX // 16, PIX // 4 + 1)
    spot_high = jax.random.randint(keys[1], (), 0, PAIRS)
    spot_low = (spot_high + 1 + jax.random.randint(keys[2], (), 0, PAIRS - 1)) % PAIRS
    slots = jnp.arange(PAIRS, dtype=jnp.int32)
    lengths = jnp.where(slots == spot_high, PIX, lengths)
    lengths = jnp.where(slots == spot_low, PIX // 4, lengths)
    return lengths.astype(jnp.int32)


def touch_ends(entries, own_key, least, largest):
    place = [jax.random.randint(jax.random.fold_in(own_key, axis), (), 0, length) for axis, length in enumerate(entries.shape)]
    main_axis = entries.shape.index(max(entries.shape))
    next_to = place[:main_axis] + [(place[main_axis] + 1) % entries.shape[main_axis]] + place[main_axis + 1:]
    return entries.at[tuple(place)].set(least).at[tuple(next_to)].set(largest)


def levels(rng, extent, cuts, least, top_value):
    gain, own = 1.0, jax.random.fold_in(rng, 6)
    for position, blocks in cuts:
        draws = jnp.exp(jax.random.uniform(jax.random.fold_in(own, position), (blocks,), jnp.float32, least / len(cuts), top_value / len(cuts)))
        gain = gain * jnp.repeat(draws, extent[position] // blocks).reshape([-1 if axis == position else 1 for axis in range(len(extent))])
    return gain


def gaussian(stream_key, dims, deviation, bound, cuts=(), kind=jnp.bfloat16):
    values = jax.random.normal(stream_key, dims, jnp.float32) * deviation
    if len(cuts) > 0:
        values = levels(stream_key, dims, cuts, -0.22, 0.18) * values
    return jnp.clip(values, min=-bound, max=bound).astype(kind)


def setup_inputs(seed: int = 0) -> dict:
    streams_of = jax.random.split(jax.random.key(seed), 13)
    return {
        "residual": draw_residual(jax.random.fold_in(streams_of[12], 71), 0),
        "direction": draw_direction(jax.random.fold_in(streams_of[12], 71), 0),
        "legendre_scalar": gaussian(streams_of[2], (ORD_PAIRS, L, PAIRS), L ** -0.5, 0.109375, ((0, 32),)),
        "legendre_plus": gaussian(streams_of[3], (ORD_PAIRS, L, PAIRS), L ** -0.5, 0.109375, ((0, 32),)),
        "legendre_minus": gaussian(streams_of[4], (ORD_PAIRS, L, PAIRS), L ** -0.5, 0.109375, ((0, 32),)),
        "prior_inverse": draw_prior_inverse(jax.random.fold_in(streams_of[12], 71), 0),
        "noise_weight": jnp.clip(jnp.exp(math.log(0.0025) - 2.30258502 * jax.random.uniform(streams_of[6], (PAIRS, 2, 3, PIX), jnp.float32) ** levels(streams_of[6], (PAIRS, 2, 3, PIX), ((0, 32),), -0.2, 0.2)), 0.00025, 0.0025),
        "order_ids": draw_order_ids(jax.random.fold_in(streams_of[12], 71), 0),
        "live_blocks": touch_ends(jax.random.randint(streams_of[8], (ORD_PAIRS, 2), 1, BLOCKS + 1), jax.random.fold_in(streams_of[8], 1), 1, BLOCKS).astype(jnp.int32),
        "cycle_assign": jax.random.permutation(streams_of[9], PAIRS).astype(jnp.int32),
        "cycle_length": draw_cycle_length(jax.random.fold_in(streams_of[12], 71), 0),
        "cycle_shift": touch_ends(jax.random.randint(streams_of[11], (PAIRS,), 0, 2), jax.random.fold_in(streams_of[11], 1), 0, 1).astype(jnp.int32),
    }


def segment_split(coeffs, order_m):
    degree = jnp.arange(L, dtype=jnp.int32)
    first_seg = degree < (L - order_m)
    zeros = jnp.zeros_like(coeffs)
    halves = jnp.stack([jnp.where(first_seg, coeffs, zeros), jnp.where(first_seg, zeros, coeffs)])
    return halves.reshape(2, coeffs.shape[0], coeffs.shape[1], L // 2, 2)


def pair_sign(order_m):
    odd_sign = jnp.where(order_m % 2 == 0, 1.0, -1.0).astype(jnp.float32)
    return jnp.stack([jnp.ones((), jnp.float32), odd_sign])


def alive_mask(alive_count, total):
    blocks = jnp.arange(total, dtype=jnp.int32) // (total // BLOCKS)
    return blocks[None, :] < alive_count[:, None]


def spin_forward(part_scalar, part_plus, part_minus, signs):
    signs = signs[:, None, None, None]

    def hemis(part, flip):
        return jnp.stack([part[:, 0] + part[:, 1], flip * signs * (part[:, 0] - part[:, 1])], axis=1)

    scalar_h = hemis(part_scalar, 1.0)
    plus_h = hemis(part_plus, 1.0)
    minus_h = hemis(part_minus, -1.0)
    q_real = -(plus_h[:, :, 0] - minus_h[:, :, 3])
    q_imag = -(plus_h[:, :, 1] + minus_h[:, :, 2])
    u_real = -(plus_h[:, :, 2] + minus_h[:, :, 1])
    u_imag = -(plus_h[:, :, 3] - minus_h[:, :, 0])
    return jnp.stack([scalar_h[:, :, 0], scalar_h[:, :, 1], q_real, q_imag, u_real, u_imag], axis=2)


def spin_inputs(grads):
    scalar_in = grads[:, :, 0:2]
    plus_in = jnp.stack([-grads[:, :, 2], -grads[:, :, 3], -grads[:, :, 4], -grads[:, :, 5]], axis=2)
    minus_in = jnp.stack([grads[:, :, 5], -grads[:, :, 4], -grads[:, :, 3], grads[:, :, 2]], axis=2)
    return scalar_in, plus_in, jnp.flip(minus_in, axis=1)


def harmonic_sums(coeffs, scalar_t, plus_t, minus_t, order_m, alive_count):
    halves = segment_split(coeffs, order_m).astype(jnp.float32)

    def contract(table, rows):
        return jnp.einsum('acsiq,iqk->aqcsk', rows, table.astype(jnp.float32).reshape(L // 2, 2, -1))

    field = spin_forward(contract(scalar_t, halves[:, 0:2]), contract(plus_t, halves[:, 2:6]),
                         contract(minus_t, halves[:, 2:6]), pair_sign(order_m))
    alive = alive_mask(alive_count, field.shape[-1])
    return jnp.where(alive[:, None, None, None, :], field, 0.0).astype(jnp.bfloat16)


def adjoint_sums(grads, scalar_t, plus_t, minus_t, order_m, alive_count):
    alive = alive_mask(alive_count, grads.shape[-1])
    grads = jnp.where(alive[:, None, None, None, :], grads, jnp.zeros_like(grads)).astype(jnp.float32)
    scalar_in, plus_in, minus_in = spin_inputs(grads)

    def contract(table, rows):
        return jnp.einsum('iqk,aqcsk->acsiq', table.astype(jnp.float32).reshape(L // 2, 2, -1), rows,
                          precision=lax.Precision.HIGHEST)

    noise = jnp.concatenate([contract(scalar_t, scalar_in),
                             contract(plus_t, plus_in) + contract(minus_t, minus_in)], axis=1)
    noise = noise.reshape(2, 6, noise.shape[2], L)
    first_seg = jnp.arange(L, dtype=jnp.int32) < (L - order_m)
    return jnp.where(first_seg, noise[0], noise[1])


def prior_apply(coeffs, prior, order_m):
    first_seg = jnp.arange(L, dtype=jnp.int32) < (L - order_m)
    doubled = jnp.concatenate([prior, prior], axis=1)
    shifted = lax.dynamic_slice_in_dim(doubled, order_m, L, 1)
    table = jnp.where(first_seg[None, :], shifted, prior)
    temper = coeffs[0:2]
    egrad = coeffs[2:4]
    bmodes = coeffs[4:6]
    return jnp.concatenate([table[0] * temper + table[1] * egrad,
                            table[1] * temper + table[2] * egrad,
                            table[3] * bmodes], axis=0)


def cycle_basis(orders, length, shift, pix):
    pixels = jnp.arange(pix, dtype=jnp.int32)
    turns = (orders[:, None] * (2 * pixels[None, :] + shift)) % (2 * length)
    angle = turns.astype(jnp.float32) * (jnp.float32(jnp.pi) / length.astype(jnp.float32))
    return jnp.stack([2.0 * jnp.cos(angle), -2.0 * jnp.sin(angle)], axis=1).astype(jnp.bfloat16)


def cycle_slot(field, orders, order_sign, length, shift, weight):
    sims = field.shape[3]
    pix = weight.shape[2]
    basis = cycle_basis(orders, length, shift, pix)
    sky_map = jnp.einsum('mhcrs,mrj->hcsj', field.reshape(-1, 2, 3, 2, sims).astype(jnp.float32),
                         basis.astype(jnp.float32))
    inside = jnp.arange(pix, dtype=jnp.int32) < length
    weighted = jnp.where(inside, sky_map * weight[:, :, None, :], 0.0).astype(jnp.bfloat16)
    back = jnp.einsum('mrj,hcsj->mhcrs', basis.astype(jnp.float32), weighted.astype(jnp.float32))
    back = back.reshape(-1, 2, 6, sims)
    signs = order_sign[:, None, None]
    return jnp.stack([back[:, 0] + signs * back[:, 1], back[:, 0] - signs * back[:, 1]], axis=1)


def reference(residual, direction, legendre_scalar, legendre_plus, legendre_minus, prior_inverse,
              noise_weight, order_ids, live_blocks, cycle_assign, cycle_length, cycle_shift):
    sims = direction.shape[2]
    coeffs = direction.astype(jnp.bfloat16)
    fields = lax.map(lambda packed: harmonic_sums(*packed),
                     (coeffs, legendre_scalar, legendre_plus, legendre_minus, order_ids, live_blocks))
    fields = fields.reshape(ORDERS, 2, 6, sims, PAIRS)
    fields = jnp.take(fields, cycle_assign, axis=4)
    all_orders = jnp.stack([order_ids, L - order_ids], axis=1).reshape(-1)
    order_sign = jnp.where((jnp.arange(ORDERS, dtype=jnp.int32) % 2 == 0) | (all_orders % 2 == 0),
                           1.0, -1.0).astype(jnp.float32)
    per_slot = jnp.moveaxis(fields, 4, 0)
    parity = lax.map(
        lambda packed: cycle_slot(packed[0], all_orders, order_sign, packed[1], packed[2], packed[3]),
        (per_slot, cycle_length, cycle_shift, noise_weight))
    inverse = jnp.zeros((PAIRS,), jnp.int32).at[cycle_assign].set(jnp.arange(PAIRS, dtype=jnp.int32))
    grads = jnp.take(jnp.moveaxis(parity, 0, 4), inverse, axis=4)
    grads = grads.reshape(ORD_PAIRS, 2, 2, 6, sims, PAIRS)
    noise_term = lax.map(lambda packed: adjoint_sums(*packed),
                         (grads, legendre_scalar, legendre_plus, legendre_minus, order_ids, live_blocks))
    prior_term = jax.vmap(prior_apply, in_axes=(0, None, 0))(direction, prior_inverse, order_ids)
    image = prior_term + noise_term
    norm_old = jnp.sum(residual * residual, axis=(0, 1, 3))
    curvature = jnp.sum(direction * image, axis=(0, 1, 3))
    step_length = norm_old / curvature
    residual_next = residual - step_length[None, None, :, None] * image
    norm_new = jnp.sum(residual_next * residual_next, axis=(0, 1, 3))
    direction_next = residual_next + (norm_new / norm_old)[None, None, :, None] * direction
    return residual_next, direction_next, step_length
```

```python
import functools

import jax
import jax.numpy as jnp
from jax import lax
from jax.experimental import pallas as pl
from jax.experimental.pallas import tpu as pltpu
from jax.sharding import PartitionSpec as P

L = 3072
BLOCKS = 4
JC = 512
PC = 512
F32 = jnp.float32
BF16 = jnp.bfloat16
NT = (((1,), (1,)), ((), ()))
MESH = pl.DeviceIdType.MESH


def dot(a, b):
    return jnp.dot(a, b, preferred_element_type=F32)


def dot_nt(a, b):
    return lax.dot_general(a, b, NT, preferred_element_type=F32)


def iota(shape, axis):
    return lax.broadcasted_iota(jnp.int32, shape, axis)


def turn(count, length):
    whole = 2 * length
    inv = 1.0 / whole.astype(F32)
    quot = jnp.floor(count.astype(F32) * inv).astype(jnp.int32)
    rest = count - quot * whole
    rest = jnp.where(rest < 0, rest + whole, rest)
    rest = jnp.where(rest >= whole, rest - whole, rest)
    t = (rest - length).astype(F32) * inv * F32(jnp.pi)
    t2 = t * t
    s = 1.0 / 6227020800.0
    for c in (-1.0 / 39916800, 1.0 / 362880, -1.0 / 5040, 1.0 / 120, -1.0 / 6, 1.0):
        s = s * t2 + c
    s = s * t
    k = 1.0 / 479001600.0
    for c in (-1.0 / 3628800, 1.0 / 40320, -1.0 / 720, 1.0 / 24, -0.5, 1.0):
        k = k * t2 + c
    return 2.0 * s * s - 1.0, -2.0 * s * k


def kernel(
    nd, slots, K, sims, pix,
    res_h, dir_h, ts_h, tp_h, tm_h, nw_h, prior_ref, ids_ref, assign_ref,
    ids_s, live_s, len_s, shift_s,
    image_h, stats_ref,
    res, drn, ts, teb, nw, E, acc_t, acc_eb, F, send1, recv1, send2, recv2,
    basis, weighted, PAR, lt, leb, prior, image, accs, psend, precv,
    in_sem, s1, r1, s2, r2, s3, r3, own_sem, out_sem,
):
    me = lax.axis_index("dev")
    rows = 4 * slots
    total_rows = rows * nd
    order_rows = 2 * nd
    cs = 3 * sims

    loads = [
        pltpu.make_async_copy(dir_h.at[0], drn, in_sem.at[0]),
        pltpu.make_async_copy(ts_h.at[0], ts, in_sem.at[1]),
        pltpu.make_async_copy(tp_h.at[0], teb.at[:, pl.ds(0, K)], in_sem.at[2]),
        pltpu.make_async_copy(tm_h.at[0], teb.at[:, pl.ds(K, K)], in_sem.at[3]),
        pltpu.make_async_copy(nw_h, nw, in_sem.at[4]),
        pltpu.make_async_copy(res_h.at[0], res, in_sem.at[5]),
    ]
    for load in loads:
        load.start()

    barrier = pltpu.get_barrier_semaphore()

    def greet(i, carry):
        pl.semaphore_signal(
            barrier, inc=1, device_id=(lax.rem(me + i, nd),), device_id_type=MESH
        )
        return carry

    lax.fori_loop(1, nd, greet, 0)

    my_m = ids_s[me]
    odd_sign = jnp.where(lax.rem(my_m, 2) == 0, F32(1.0), F32(-1.0))

    onehot_t = (iota((K, K), 0) == assign_ref[...]).astype(F32).astype(BF16)

    def build_e(c, carry):
        r0 = c * 128
        row = iota((128, K), 0) + r0
        pick = (row // 4 == iota((128, K), 1)).astype(F32).astype(BF16)
        block = dot_nt(pick, onehot_t)
        for oh in range(4):
            E[pl.ds(pl.multiple_of(r0, 128), 128), oh * K : (oh + 1) * K] = jnp.where(
                row % 4 == oh, block, 0.0
            ).astype(BF16)
        return carry

    lax.fori_loop(0, total_rows // 128, build_e, 0)

    for load in loads[:4]:
        load.wait()

    def lane_masks(j0):
        lane = iota((1, JC), 1) + j0
        return lane < L - my_m, lane % 2 == 0

    for c in range(L // JC):
        first, even = lane_masks(c * JC)
        alt = jnp.where(even, 1.0, -1.0)
        m0 = first.astype(F32)
        m1 = 1.0 - m0
        x = drn[:, :, c * JC : (c + 1) * JC].reshape(6 * sims, JC)
        parts = [(x * m).astype(BF16) for m in (m0, m0 * alt, m1, m1 * alt)]
        lhs_t = jnp.concatenate([p[: 2 * sims] for p in parts], axis=0)
        lhs_eb = jnp.concatenate([p[2 * sims :] for p in parts], axis=0)
        add_t = dot(lhs_t, ts[c * JC : (c + 1) * JC, :])
        add_eb = dot(lhs_eb, teb[c * JC : (c + 1) * JC, :])
        if c == 0:
            acc_t[...] = add_t
            acc_eb[...] = add_eb
        else:
            acc_t[...] += add_t
            acc_eb[...] += add_eb

    def alive(s, height):
        return iota((height, K), 1) // (K // BLOCKS) < live_s[0, s]

    for s in range(2):
        g = F32(1.0) if s == 0 else odd_sign
        live = alive(s, sims)
        for h in range(2):
            a = 2 * s + h
            sg = F32(1.0) if h == 0 else g
            sx = F32(1.0) if h == 0 else -g
            t0 = 2 * sims * a
            e0 = 4 * sims * a
            t_re = sg * acc_t[t0 : t0 + sims, :]
            t_im = sg * acc_t[t0 + sims : t0 + 2 * sims, :]
            w = [sg * acc_eb[e0 + i * sims : e0 + (i + 1) * sims, 0:K] for i in range(4)]
            v = [sx * acc_eb[e0 + i * sims : e0 + (i + 1) * sims, K : 2 * K] for i in range(4)]
            zero = jnp.zeros((sims, K), F32)
            blocks = [
                t_re, v[3] - w[0], -(w[2] + v[1]), zero,
                t_im, -(w[1] + v[2]), v[0] - w[3], zero,
            ]
            for i, block in enumerate(blocks):
                F[i * sims : (i + 1) * sims, a * K : (a + 1) * K] = jnp.where(
                    live, block, 0.0
                ).astype(BF16)

    CH = min(512, total_rows)

    def fill1(c, carry):
        at = pl.ds(pl.multiple_of(c * CH, CH), CH)
        send1[at, :] = dot_nt(E[at, :], F[...]).astype(BF16)
        return carry

    lax.fori_loop(0, total_rows // CH, fill1, 0)

    pl.semaphore_wait(barrier, nd - 1)

    def block_at(ref, d, size):
        return ref.at[pl.ds(pl.multiple_of(d * size, size), size)]

    def remote(send, recv, ss, rs, i, size):
        dst = lax.rem(me + i, nd)
        return pltpu.make_async_remote_copy(
            src_ref=send if size is None else block_at(send, dst, size),
            dst_ref=recv.at[me] if size is None else block_at(recv, me, size),
            send_sem=ss.at[i],
            recv_sem=rs.at[i],
            device_id=(dst,),
            device_id_type=MESH,
        )

    def start_all(*args):
        def go(i, carry):
            remote(*args[:4], i, args[4]).start()
            return carry

        lax.fori_loop(1, nd, go, 0)

    def wait_recv_all(*args):
        def go(i, carry):
            remote(*args[:4], i, args[4]).wait_recv()
            return carry

        lax.fori_loop(1, nd, go, 0)

    def wait_send_all(*args):
        def go(i, carry):
            remote(*args[:4], i, args[4]).wait_send()
            return carry

        lax.fori_loop(1, nd, go, 0)

    def own(send, recv, i):
        return pltpu.make_async_copy(
            block_at(send, me, rows), block_at(recv, me, rows), own_sem.at[i]
        )

    ex1 = (send1, recv1, s1, r1, rows)
    start_all(*ex1)
    own(send1, recv1, 0).start()

    ids = ids_ref[...].astype(F32)
    OB = min(64, order_rows)
    for ob in range(order_rows // OB):
        row = iota((OB, nd), 0) + ob * OB
        m_col = jnp.sum(
            jnp.where(iota((OB, nd), 1) == row // 2, ids, 0.0), axis=1, keepdims=True
        ).astype(jnp.int32)
        m_full = jnp.broadcast_to(m_col, (OB, 128))
        m_full = jnp.where(iota((OB, 128), 0) % 2 == 0, m_full, L - m_full)
        for tl in range(slots):
            n_full = jnp.full((OB, 128), len_s[tl], jnp.int32)
            spot = 2 * iota((OB, 128), 1) + shift_s[tl]
            co, si = turn(m_full * spot, n_full)
            wc, ws = turn(m_full * 256, n_full)

            def step(a, carry, tl=tl, ob=ob, wc=wc, ws=ws):
                re, im = carry
                at = pl.ds(pl.multiple_of(a * 128, 128), 128)
                basis[tl, ob * OB : (ob + 1) * OB, at] = re.astype(BF16)
                basis[tl, order_rows + ob * OB : order_rows + (ob + 1) * OB, at] = im.astype(BF16)
                return re * wc + im * ws, im * wc - re * ws

            lax.fori_loop(0, pix // 128, step, (2.0 * co, -2.0 * si))

    lane = iota((1, 2 * order_rows), 1)
    spread = (iota((nd, 2 * order_rows), 0) == (lane % order_rows) // 2).astype(F32)
    odd = dot(jnp.broadcast_to((ids_ref[...] % 2).astype(F32), (8, nd)), spread)[0:1]
    g_row = jnp.where((odd > 0.5) & (lane % 2 == 1), -1.0, 1.0)

    pr = prior_ref[...]
    sigma = jnp.maximum(jnp.max(jnp.abs(pr)), 1.0)
    pr8 = jnp.concatenate([pr, pr], axis=0)
    rolled = pltpu.roll(pr8, L - my_m, 1)
    first_row = iota((8, L), 1) < L - my_m
    prior[...] = jnp.where(first_row, rolled, pr8)
    inv_sigma = 1.0 / jnp.full((sims, 128), sigma, F32)

    loads[4].wait()
    loads[5].wait()

    def fold(x):
        x = x[0] + x[1] + x[2] + x[3] + x[4] + x[5]
        out = x[:, 0:128]
        for i in range(1, x.shape[1] // 128):
            out = out + x[:, i * 128 : (i + 1) * 128]
        return out

    norm = jnp.zeros((sims, 128), F32)
    for c in range(L // JC):
        x = res[:, :, c * JC : (c + 1) * JC]
        norm = norm + fold(x * x)
    accs[0:sims, :] = norm
    accs[sims : 4 * sims, :] = jnp.zeros((3 * sims, 128), F32)

    own(send1, recv1, 0).wait()
    wait_recv_all(*ex1)

    def slot(tl, carry):
        a = iota((2 * order_rows, total_rows), 0)
        want = ((a // 2) % nd) * rows + tl * 4 + (a % 2) * 2 + a // order_rows
        sel = (iota((2 * order_rows, total_rows), 1) == want).astype(F32).astype(BF16)
        D = dot(sel, recv1[...])
        mt = jnp.concatenate(
            [
                jnp.concatenate([D[0:order_rows, 0:128], D[order_rows:, 0:128]], axis=1),
                jnp.concatenate([D[0:order_rows, 128:256], D[order_rows:, 128:256]], axis=1),
            ],
            axis=0,
        )
        mm = mt.T
        M = jnp.concatenate([mm[0:cs], mm[128 : 128 + cs]], axis=0).astype(BF16)
        n = len_s[tl]
        for c in range(pix // PC):
            at = slice(c * PC, (c + 1) * PC)
            sky = dot(M, basis[tl, :, at]).reshape(2, 3, sims, PC)
            inside = iota((2, 3, PC), 2) + c * PC < n
            wt = jnp.where(inside, nw[tl, :, :, at], 0.0)
            weighted[:, at] = (sky * wt[:, :, None, :]).reshape(2 * cs, PC).astype(BF16)
        back = dot_nt(weighted[...], basis[tl])
        north = back[0:cs]
        south = back[cs : 2 * cs] * g_row
        pad = jnp.zeros((128 - cs, 2 * order_rows), F32)
        for q, par in enumerate((north + south, north - south)):
            pt = jnp.concatenate([par, pad], axis=0).T.astype(BF16)
            at = pl.ds(pl.multiple_of((tl * 2 + q) * order_rows, order_rows), order_rows)
            PAR[at, 0:128] = pt[0:order_rows]
            PAR[at, 128:256] = pt[order_rows:]
        return carry

    lax.fori_loop(0, slots, slot, 0)

    def fill2(c, carry):
        at = pl.ds(pl.multiple_of(c * CH, CH), CH)
        b = iota((CH, total_rows), 0) + c * CH
        want = ((((b // 4) % slots) * 2 + b % 2) * nd + b // rows) * 2 + (b // 2) % 2
        sel = (iota((CH, total_rows), 1) == want).astype(F32).astype(BF16)
        send2[at, :] = dot(sel, PAR[...]).astype(BF16)
        return carry

    lax.fori_loop(0, total_rows // CH, fill2, 0)

    ex2 = (send2, recv2, s2, r2, rows)
    start_all(*ex2)
    own(send2, recv2, 1).start()
    wait_send_all(*ex1)
    own(send2, recv2, 1).wait()
    wait_recv_all(*ex2)

    GT = dot(recv2[...].astype(F32).T.astype(BF16), E[...])
    for s in range(2):
        live = alive(s, 256)
        G = [
            jnp.where(live, GT[:, (2 * s + q) * K : (2 * s + q + 1) * K], 0.0) for q in range(2)
        ]
        for q in range(2):
            a = 2 * s + q
            A, B = G[q], G[1 - q]
            lt[2 * sims * a : 2 * sims * a + sims, :] = A[0:sims].astype(BF16)
            lt[2 * sims * a + sims : 2 * sims * (a + 1), :] = A[128 : 128 + sims].astype(BF16)
            qr, ur = slice(sims, 2 * sims), slice(2 * sims, 3 * sims)
            qi, ui = slice(128 + sims, 128 + 2 * sims), slice(128 + 2 * sims, 128 + 3 * sims)
            plus = (-A[qr], -A[qi], -A[ur], -A[ui])
            minus = (B[ui], -B[ur], -B[qi], B[qr])
            for i in range(4):
                e0 = 4 * sims * a + i * sims
                leb[e0 : e0 + sims, 0:K] = plus[i].astype(BF16)
                leb[e0 : e0 + sims, K : 2 * K] = minus[i].astype(BF16)

    outs = []
    for c in range(L // JC):
        at = slice(c * JC, (c + 1) * JC)
        first, even = lane_masks(c * JC)
        nt = dot_nt(lt[...], ts[at, :])
        ne = dot_nt(leb[...], teb[at, :])

        def choose(x, size):
            x = [x[i * size : (i + 1) * size] for i in range(4)]
            return jnp.where(
                first, jnp.where(even, x[0], x[1]), jnp.where(even, x[2], x[3])
            )

        nt = choose(nt, 2 * sims).reshape(2, sims, JC)
        ne = choose(ne, 4 * sims).reshape(4, sims, JC)
        tt, te, ee, bb = [prior[i : i + 1, at][None] for i in range(4)]
        d = drn[:, :, at]
        img = jnp.concatenate(
            [
                nt + tt * d[0:2] + te * d[2:4],
                ne[0:2] + te * d[0:2] + ee * d[2:4],
                ne[2:4] + bb * d[4:6],
            ],
            axis=0,
        )
        image[:, :, at] = img
        out = pltpu.make_async_copy(image.at[:, :, at], image_h.at[0, :, :, at], out_sem.at[c])
        out.start()
        outs.append(out)
        scaled = img * inv_sigma[0:1, 0:1][None]
        accs[sims : 2 * sims, :] += fold(d * scaled)
        accs[2 * sims : 3 * sims, :] += fold(res[:, :, at] * scaled)
        accs[3 * sims : 4 * sims, :] += fold(scaled * scaled)

    local = jnp.sum(accs[...].T, axis=0, keepdims=True)
    psend[...] = jnp.broadcast_to(local, (8, 4 * sims))
    precv[me] = psend[...]
    ex3 = (psend, precv, s3, r3, None)
    start_all(*ex3)
    for out in outs:
        out.wait()
    wait_send_all(*ex2)
    wait_recv_all(*ex3)
    total = precv[0]
    for i in range(1, nd):
        total = total + precv[i]
    stats_ref[0:8, :] = total
    stats_ref[8:16, :] = jnp.full((8, 4 * sims), sigma, F32)
    wait_send_all(*ex3)


def body(
    residual, direction, legendre_scalar, legendre_plus, legendre_minus, prior_inverse,
    noise_weight, order_ids, live_blocks, cycle_assign, cycle_length, cycle_shift, nd,
):
    sims = direction.shape[2]
    K = legendre_scalar.shape[2]
    slots = cycle_length.shape[0]
    pix = noise_weight.shape[3]
    assert direction.shape[0] == 1
    rows = 4 * slots
    total_rows = rows * nd
    vmem = pl.BlockSpec(memory_space=pltpu.VMEM)
    smem = pl.BlockSpec(memory_space=pltpu.SMEM)
    hbm = pl.BlockSpec(memory_space=pl.ANY)
    dma = pltpu.SemaphoreType.DMA
    image, stats = pl.pallas_call(
        functools.partial(kernel, nd, slots, K, sims, pix),
        out_shape=(
            jax.ShapeDtypeStruct(direction.shape, F32),
            jax.ShapeDtypeStruct((16, 4 * sims), F32),
        ),
        in_specs=[hbm] * 6 + [vmem] * 3 + [smem] * 4,
        out_specs=(hbm, vmem),
        scratch_shapes=[
            pltpu.VMEM((6, sims, L), F32),
            pltpu.VMEM((6, sims, L), F32),
            pltpu.VMEM((L, K), BF16),
            pltpu.VMEM((L, 2 * K), BF16),
            pltpu.VMEM((slots, 2, 3, pix), F32),
            pltpu.VMEM((total_rows, 4 * K), BF16),
            pltpu.VMEM((8 * sims, K), F32),
            pltpu.VMEM((16 * sims, 2 * K), F32),
            pltpu.VMEM((256, 4 * K), BF16),
            pltpu.VMEM((total_rows, 256), BF16),
            pltpu.VMEM((total_rows, 256), BF16),
            pltpu.VMEM((total_rows, 256), BF16),
            pltpu.VMEM((total_rows, 256), BF16),
            pltpu.VMEM((slots, 4 * nd, pix), BF16),
            pltpu.VMEM((6 * sims, pix), BF16),
            pltpu.VMEM((total_rows, 256), BF16),
            pltpu.VMEM((8 * sims, K), BF16),
            pltpu.VMEM((16 * sims, 2 * K), BF16),
            pltpu.VMEM((8, L), F32),
            pltpu.VMEM((6, sims, L), F32),
            pltpu.VMEM((4 * sims, 128), F32),
            pltpu.VMEM((8, 4 * sims), F32),
            pltpu.VMEM((nd, 8, 4 * sims), F32),
            dma((6,)), dma((nd,)), dma((nd,)), dma((nd,)), dma((nd,)), dma((nd,)), dma((nd,)),
            dma((2,)), dma((L // JC,)),
        ],
        compiler_params=pltpu.CompilerParams(
            collective_id=0, has_side_effects=True, vmem_limit_bytes=60 * 1024 * 1024
        ),
        name="cg",
    )(
        residual, direction, legendre_scalar, legendre_plus, legendre_minus, noise_weight,
        prior_inverse, order_ids.reshape(1, -1), cycle_assign.reshape(1, -1),
        order_ids, live_blocks, cycle_length, cycle_shift,
    )
    norm_old, da, ra, aa = [stats[0, i * sims : (i + 1) * sims] for i in range(4)]
    scaled_step = norm_old / da
    step_length = scaled_step / stats[8, 0:sims]
    norm_new = norm_old - 2.0 * scaled_step * ra + scaled_step * scaled_step * aa
    ratio = norm_new / norm_old
    residual_next = residual - step_length[None, None, :, None] * image
    direction_next = residual_next + ratio[None, None, :, None] * direction
    return (residual_next, direction_next, step_length)


def solution(mesh):
    return jax.shard_map(
        functools.partial(body, nd=mesh.shape["dev"]),
        mesh=mesh,
        in_specs=(
            P("dev", None, None, None),
            P("dev", None, None, None),
            P("dev", None, None),
            P("dev", None, None),
            P("dev", None, None),
            P(),
            P("dev", None, None, None),
            P(),
            P("dev", None),
            P(),
            P("dev"),
            P("dev"),
        ),
        out_specs=(P("dev", None, None, None), P("dev", None, None, None), P()),
        check_vma=False,
    )
```

```python
import functools

import jax
import jax.numpy as jnp
from jax import lax
from jax.experimental import pallas as pl
from jax.experimental.pallas import tpu as pltpu
from jax.sharding import PartitionSpec as P

L = 3072
BLOCKS = 4
JC = 512
PC = 512
F32 = jnp.float32
BF16 = jnp.bfloat16
NT = (((1,), (1,)), ((), ()))
MESH = pl.DeviceIdType.MESH


def dot(a, b):
    return jnp.dot(a, b, preferred_element_type=F32)


def dot_nt(a, b):
    return lax.dot_general(a, b, NT, preferred_element_type=F32)


def iota(shape, axis):
    return lax.broadcasted_iota(jnp.int32, shape, axis)


def turn(count, length):
    whole = 2 * length
    inv = 1.0 / whole.astype(F32)
    quot = jnp.floor(count.astype(F32) * inv).astype(jnp.int32)
    rest = count - quot * whole
    rest = jnp.where(rest < 0, rest + whole, rest)
    rest = jnp.where(rest >= whole, rest - whole, rest)
    t = (rest - length).astype(F32) * inv * F32(jnp.pi)
    t2 = t * t
    s = 1.0 / 6227020800.0
    for c in (-1.0 / 39916800, 1.0 / 362880, -1.0 / 5040, 1.0 / 120, -1.0 / 6, 1.0):
        s = s * t2 + c
    s = s * t
    k = 1.0 / 479001600.0
    for c in (-1.0 / 3628800, 1.0 / 40320, -1.0 / 720, 1.0 / 24, -0.5, 1.0):
        k = k * t2 + c
    return 2.0 * s * s - 1.0, -2.0 * s * k


def kernel(
    nd, slots, K, sims, pix,
    res_h, dir_h, ts_h, tp_h, tm_h, nw_h, prior_ref, ids_ref, assign_ref,
    ids_s, live_s, len_s, shift_s,
    image_h, stats_ref,
    res, drn, ts, teb, nw, E, acc_t, acc_eb, F, send1, recv1, send2, recv2,
    basis, weighted, PAR, lt, leb, prior, image, accs, psend, precv,
    in_sem, s1, r1, s2, r2, s3, r3, own_sem, out_sem,
):
    me = lax.axis_index("dev")
    groups = slots // 2
    half = 8 * nd
    total_rows = half * groups
    order_rows = 2 * nd
    cs = 3 * sims

    loads = [
        pltpu.make_async_copy(dir_h.at[0], drn, in_sem.at[0]),
        pltpu.make_async_copy(ts_h.at[0], ts, in_sem.at[1]),
        pltpu.make_async_copy(tp_h.at[0], teb.at[:, pl.ds(0, K)], in_sem.at[2]),
        pltpu.make_async_copy(tm_h.at[0], teb.at[:, pl.ds(K, K)], in_sem.at[3]),
        pltpu.make_async_copy(nw_h, nw, in_sem.at[4]),
        pltpu.make_async_copy(res_h.at[0], res, in_sem.at[5]),
    ]
    for load in loads:
        load.start()

    barrier = pltpu.get_barrier_semaphore()

    def greet(i, carry):
        pl.semaphore_signal(
            barrier, inc=1, device_id=(lax.rem(me + i, nd),), device_id_type=MESH
        )
        return carry

    lax.fori_loop(1, nd, greet, 0)

    my_m = ids_s[me]
    odd_sign = jnp.where(lax.rem(my_m, 2) == 0, F32(1.0), F32(-1.0))

    onehot_t = (iota((K, K), 0) == assign_ref[...]).astype(F32).astype(BF16)

    def build_e(c, carry):
        r0 = c * 128
        row = iota((128, K), 0) + r0
        cycle = (row // 8) % nd * slots + row // half * 2 + (row // 4) % 2
        pick = (cycle == iota((128, K), 1)).astype(F32).astype(BF16)
        block = dot_nt(pick, onehot_t)
        for oh in range(4):
            E[pl.ds(pl.multiple_of(r0, 128), 128), oh * K : (oh + 1) * K] = jnp.where(
                row % 4 == oh, block, 0.0
            ).astype(BF16)
        return carry

    lax.fori_loop(0, total_rows // 128, build_e, 0)

    for load in loads[:4]:
        load.wait()

    def lane_masks(j0):
        lane = iota((1, JC), 1) + j0
        return lane < L - my_m, lane % 2 == 0

    for c in range(L // JC):
        first, even = lane_masks(c * JC)
        alt = jnp.where(even, 1.0, -1.0)
        m0 = first.astype(F32)
        m1 = 1.0 - m0
        x = drn[:, :, c * JC : (c + 1) * JC].reshape(6 * sims, JC)
        parts = [(x * m).astype(BF16) for m in (m0, m0 * alt, m1, m1 * alt)]
        lhs_t = jnp.concatenate([p[: 2 * sims] for p in parts], axis=0)
        lhs_eb = jnp.concatenate([p[2 * sims :] for p in parts], axis=0)
        add_t = dot(lhs_t, ts[c * JC : (c + 1) * JC, :])
        add_eb = dot(lhs_eb, teb[c * JC : (c + 1) * JC, :])
        if c == 0:
            acc_t[...] = add_t
            acc_eb[...] = add_eb
        else:
            acc_t[...] += add_t
            acc_eb[...] += add_eb

    def alive(s, height):
        return iota((height, K), 1) // (K // BLOCKS) < live_s[0, s]

    for s in range(2):
        g = F32(1.0) if s == 0 else odd_sign
        live = alive(s, sims)
        for h in range(2):
            a = 2 * s + h
            sg = F32(1.0) if h == 0 else g
            sx = F32(1.0) if h == 0 else -g
            t0 = 2 * sims * a
            e0 = 4 * sims * a
            t_re = sg * acc_t[t0 : t0 + sims, :]
            t_im = sg * acc_t[t0 + sims : t0 + 2 * sims, :]
            w = [sg * acc_eb[e0 + i * sims : e0 + (i + 1) * sims, 0:K] for i in range(4)]
            v = [sx * acc_eb[e0 + i * sims : e0 + (i + 1) * sims, K : 2 * K] for i in range(4)]
            zero = jnp.zeros((sims, K), F32)
            blocks = [
                t_re, v[3] - w[0], -(w[2] + v[1]), zero,
                t_im, -(w[1] + v[2]), v[0] - w[3], zero,
            ]
            for i, block in enumerate(blocks):
                F[i * sims : (i + 1) * sims, a * K : (a + 1) * K] = jnp.where(
                    live, block, 0.0
                ).astype(BF16)

    def pack(x):
        parts = [x[:, 0:128].reshape(nd, 8, 128), x[:, 128:256].reshape(nd, 8, 128)]
        return jnp.concatenate(parts, axis=1).astype(BF16)

    def unpack(x):
        x = x.astype(F32)
        parts = [x[:, 0:8].reshape(half, 128), x[:, 8:16].reshape(half, 128)]
        return jnp.concatenate(parts, axis=1)

    def remote(send, recv, ss, rs, g, i):
        dst = lax.rem(me + i, nd)
        return pltpu.make_async_remote_copy(
            src_ref=send if g is None else send.at[g, dst],
            dst_ref=recv.at[me] if g is None else recv.at[g, me],
            send_sem=ss.at[i] if g is None else ss.at[g, i],
            recv_sem=rs.at[i] if g is None else rs.at[g, i],
            device_id=(dst,),
            device_id_type=MESH,
        )

    def start_all(*args):
        def go(i, carry):
            remote(*args, i).start()
            return carry

        lax.fori_loop(1, nd, go, 0)

    def wait_recv_all(*args):
        def go(i, carry):
            remote(*args, i).wait_recv()
            return carry

        lax.fori_loop(1, nd, go, 0)

    def wait_send_all(*args):
        def go(i, carry):
            remote(*args, i).wait_send()
            return carry

        lax.fori_loop(1, nd, go, 0)

    def own(send, recv, e, g):
        return pltpu.make_async_copy(send.at[g, me], recv.at[g, me], own_sem.at[e, g])

    ex1 = (send1, recv1, s1, r1)
    ex2 = (send2, recv2, s2, r2)
    for g in range(groups):
        send1[g] = pack(dot_nt(E[g * half : (g + 1) * half, :], F[...]))
        if g == 0:
            pl.semaphore_wait(barrier, nd - 1)
        start_all(*ex1, g)
        own(send1, recv1, 0, g).start()

    ids = ids_ref[...].astype(F32)
    OB = min(64, order_rows)
    for ob in range(order_rows // OB):
        row = iota((OB, nd), 0) + ob * OB
        m_col = jnp.sum(
            jnp.where(iota((OB, nd), 1) == row // 2, ids, 0.0), axis=1, keepdims=True
        ).astype(jnp.int32)
        m_full = jnp.broadcast_to(m_col, (OB, 128))
        m_full = jnp.where(iota((OB, 128), 0) % 2 == 0, m_full, L - m_full)
        for tl in range(slots):
            n_full = jnp.full((OB, 128), len_s[tl], jnp.int32)
            spot = 2 * iota((OB, 128), 1) + shift_s[tl]
            co, si = turn(m_full * spot, n_full)
            wc, ws = turn(m_full * 256, n_full)

            def step(a, carry, tl=tl, ob=ob, wc=wc, ws=ws):
                re, im = carry
                at = pl.ds(pl.multiple_of(a * 128, 128), 128)
                basis[tl, ob * OB : (ob + 1) * OB, at] = re.astype(BF16)
                basis[tl, order_rows + ob * OB : order_rows + (ob + 1) * OB, at] = im.astype(BF16)
                return re * wc + im * ws, im * wc - re * ws

            lax.fori_loop(0, pix // 128, step, (2.0 * co, -2.0 * si))

    lane = iota((1, 2 * order_rows), 1)
    spread = (iota((nd, 2 * order_rows), 0) == (lane % order_rows) // 2).astype(F32)
    odd = dot(jnp.broadcast_to((ids_ref[...] % 2).astype(F32), (8, nd)), spread)[0:1]
    g_row = jnp.where((odd > 0.5) & (lane % 2 == 1), -1.0, 1.0)

    loads[4].wait()

    def slot(tl, D):
        mt = jnp.concatenate(
            [
                jnp.concatenate([D[0:order_rows, 0:128], D[order_rows:, 0:128]], axis=1),
                jnp.concatenate([D[0:order_rows, 128:256], D[order_rows:, 128:256]], axis=1),
            ],
            axis=0,
        )
        mm = mt.T
        M = jnp.concatenate([mm[0:cs], mm[128 : 128 + cs]], axis=0).astype(BF16)
        n = len_s[tl]
        for c in range(pix // PC):
            at = slice(c * PC, (c + 1) * PC)
            sky = dot(M, basis[tl, :, at]).reshape(2, 3, sims, PC)
            inside = iota((3, 2, PC), 2) + c * PC < n
            wt = jnp.where(inside, nw[tl, :, :, at], 0.0)
            for h in range(2):
                part = sky[h] * wt[:, h : h + 1, :]
                weighted[h * cs : (h + 1) * cs, at] = part.reshape(cs, PC).astype(BF16)
        back = dot_nt(weighted[...], basis[tl])
        north = back[0:cs]
        south = back[cs : 2 * cs] * g_row
        pad = jnp.zeros((128 - cs, 2 * order_rows), F32)
        for q, par in enumerate((north + south, north - south)):
            pt = jnp.concatenate([par, pad], axis=0).T.astype(BF16)
            r0 = ((tl % 2) * 2 + q) * order_rows
            PAR[r0 : r0 + order_rows, 0:128] = pt[0:order_rows]
            PAR[r0 : r0 + order_rows, 128:256] = pt[order_rows:]

    a = iota((half, half), 0)
    want = (a // 2) % nd * 8 + a // (4 * nd) * 4 + a % 2 * 2 + a // (2 * nd) % 2
    gather = (iota((half, half), 1) == want).astype(F32).astype(BF16)
    want = ((a // 4 % 2 * 2 + a % 2) * nd + a // 8) * 2 + a // 2 % 2
    scatter = (iota((half, half), 1) == want).astype(F32).astype(BF16)
    for g in range(groups):
        own(send1, recv1, 0, g).wait()
        wait_recv_all(*ex1, g)
        D = dot(gather, unpack(recv1[g]).astype(BF16))
        for i in range(2):
            slot(2 * g + i, D[2 * i * order_rows : 2 * (i + 1) * order_rows])
        send2[g] = pack(dot(scatter, PAR[...]))
        start_all(*ex2, g)
        own(send2, recv2, 1, g).start()

    pr = prior_ref[...]
    sigma = jnp.maximum(jnp.max(jnp.abs(pr)), 1.0)
    pr8 = jnp.concatenate([pr, pr], axis=0)
    rolled = pltpu.roll(pr8, L - my_m, 1)
    first_row = iota((8, L), 1) < L - my_m
    prior[...] = jnp.where(first_row, rolled, pr8)
    inv_sigma = 1.0 / jnp.full((sims, 128), sigma, F32)

    loads[5].wait()

    def fold(x):
        x = x[0] + x[1] + x[2] + x[3] + x[4] + x[5]
        out = x[:, 0:128]
        for i in range(1, x.shape[1] // 128):
            out = out + x[:, i * 128 : (i + 1) * 128]
        return out

    norm = jnp.zeros((sims, 128), F32)
    for c in range(L // JC):
        x = res[:, :, c * JC : (c + 1) * JC]
        norm = norm + fold(x * x)
    accs[0:sims, :] = norm
    accs[sims : 4 * sims, :] = jnp.zeros((3 * sims, 128), F32)

    for g in range(groups):
        wait_send_all(*ex1, g)

    GT = None
    for g in range(groups):
        own(send2, recv2, 1, g).wait()
        wait_recv_all(*ex2, g)
        add = dot(unpack(recv2[g]).T.astype(BF16), E[g * half : (g + 1) * half, :])
        GT = add if GT is None else GT + add
    for s in range(2):
        live = alive(s, 256)
        G = [
            jnp.where(live, GT[:, (2 * s + q) * K : (2 * s + q + 1) * K], 0.0) for q in range(2)
        ]
        for q in range(2):
            a = 2 * s + q
            A, B = G[q], G[1 - q]
            lt[2 * sims * a : 2 * sims * a + sims, :] = A[0:sims].astype(BF16)
            lt[2 * sims * a + sims : 2 * sims * (a + 1), :] = A[128 : 128 + sims].astype(BF16)
            qr, ur = slice(sims, 2 * sims), slice(2 * sims, 3 * sims)
            qi, ui = slice(128 + sims, 128 + 2 * sims), slice(128 + 2 * sims, 128 + 3 * sims)
            plus = (-A[qr], -A[qi], -A[ur], -A[ui])
            minus = (B[ui], -B[ur], -B[qi], B[qr])
            for i in range(4):
                e0 = 4 * sims * a + i * sims
                leb[e0 : e0 + sims, 0:K] = plus[i].astype(BF16)
                leb[e0 : e0 + sims, K : 2 * K] = minus[i].astype(BF16)

    outs = []
    for c in range(L // JC):
        at = slice(c * JC, (c + 1) * JC)
        first, even = lane_masks(c * JC)
        nt = dot_nt(lt[...], ts[at, :])
        ne = dot_nt(leb[...], teb[at, :])

        def choose(x, size):
            x = [x[i * size : (i + 1) * size] for i in range(4)]
            return jnp.where(
                first, jnp.where(even, x[0], x[1]), jnp.where(even, x[2], x[3])
            )

        nt = choose(nt, 2 * sims).reshape(2, sims, JC)
        ne = choose(ne, 4 * sims).reshape(4, sims, JC)
        tt, te, ee, bb = [prior[i : i + 1, at][None] for i in range(4)]
        d = drn[:, :, at]
        img = jnp.concatenate(
            [
                nt + tt * d[0:2] + te * d[2:4],
                ne[0:2] + te * d[0:2] + ee * d[2:4],
                ne[2:4] + bb * d[4:6],
            ],
            axis=0,
        )
        image[:, :, at] = img
        out = pltpu.make_async_copy(image.at[:, :, at], image_h.at[0, :, :, at], out_sem.at[c])
        out.start()
        outs.append(out)
        scaled = img * inv_sigma[0:1, 0:1][None]
        accs[sims : 2 * sims, :] += fold(d * scaled)
        accs[2 * sims : 3 * sims, :] += fold(res[:, :, at] * scaled)
        accs[3 * sims : 4 * sims, :] += fold(scaled * scaled)

    local = jnp.sum(accs[...].T, axis=0, keepdims=True)
    psend[...] = jnp.broadcast_to(local, (8, 4 * sims))
    precv[me] = psend[...]
    ex3 = (psend, precv, s3, r3, None)
    start_all(*ex3)
    for out in outs:
        out.wait()
    for g in range(groups):
        wait_send_all(*ex2, g)
    wait_recv_all(*ex3)
    total = precv[0]
    for i in range(1, nd):
        total = total + precv[i]
    stats_ref[0 : 4 * sims, :] = jnp.broadcast_to(total.T[:, 0:1], (4 * sims, 128))
    stats_ref[4 * sims : 5 * sims, :] = jnp.full((sims, 128), sigma, F32)
    wait_send_all(*ex3)


def update(sims, stats, res, drn, img, res_out, dir_out, step_out):
    norm_old, da, ra, aa, sigma = [stats[i * sims : (i + 1) * sims, :] for i in range(5)]
    scaled = norm_old / da
    step = scaled / sigma
    ratio = (norm_old - 2.0 * scaled * ra + scaled * scaled * aa) / norm_old
    step_out[...] = step.T[0:1, :]
    after = res[0, 0] - step[:, 0:1] * img[0, 0]
    res_out[0, 0] = after
    dir_out[0, 0] = after + ratio[:, 0:1] * drn[0, 0]


def body(
    residual, direction, legendre_scalar, legendre_plus, legendre_minus, prior_inverse,
    noise_weight, order_ids, live_blocks, cycle_assign, cycle_length, cycle_shift, nd,
):
    sims = direction.shape[2]
    K = legendre_scalar.shape[2]
    slots = cycle_length.shape[0]
    pix = noise_weight.shape[3]
    assert direction.shape[0] == 1
    assert slots % 2 == 0
    groups = slots // 2
    half = 8 * nd
    total_rows = half * groups
    vmem = pl.BlockSpec(memory_space=pltpu.VMEM)
    smem = pl.BlockSpec(memory_space=pltpu.SMEM)
    hbm = pl.BlockSpec(memory_space=pl.ANY)
    dma = pltpu.SemaphoreType.DMA
    image, stats = pl.pallas_call(
        functools.partial(kernel, nd, slots, K, sims, pix),
        out_shape=(
            jax.ShapeDtypeStruct(direction.shape, F32),
            jax.ShapeDtypeStruct((5 * sims, 128), F32),
        ),
        in_specs=[hbm] * 6 + [vmem] * 3 + [smem] * 4,
        out_specs=(hbm, vmem),
        scratch_shapes=[
            pltpu.VMEM((6, sims, L), F32),
            pltpu.VMEM((6, sims, L), F32),
            pltpu.VMEM((L, K), BF16),
            pltpu.VMEM((L, 2 * K), BF16),
            pltpu.VMEM((slots, 3, 2, pix), F32),
            pltpu.VMEM((total_rows, 4 * K), BF16),
            pltpu.VMEM((8 * sims, K), F32),
            pltpu.VMEM((16 * sims, 2 * K), F32),
            pltpu.VMEM((256, 4 * K), BF16),
            pltpu.VMEM((groups, nd, 16, 128), BF16),
            pltpu.VMEM((groups, nd, 16, 128), BF16),
            pltpu.VMEM((groups, nd, 16, 128), BF16),
            pltpu.VMEM((groups, nd, 16, 128), BF16),
            pltpu.VMEM((slots, 4 * nd, pix), BF16),
            pltpu.VMEM((6 * sims, pix), BF16),
            pltpu.VMEM((half, 256), BF16),
            pltpu.VMEM((8 * sims, K), BF16),
            pltpu.VMEM((16 * sims, 2 * K), BF16),
            pltpu.VMEM((8, L), F32),
            pltpu.VMEM((6, sims, L), F32),
            pltpu.VMEM((4 * sims, 128), F32),
            pltpu.VMEM((8, 4 * sims), F32),
            pltpu.VMEM((nd, 8, 4 * sims), F32),
            dma((6,)), *[dma((groups, nd))] * 4, dma((nd,)), dma((nd,)),
            dma((2, groups)), dma((L // JC,)),
        ],
        compiler_params=pltpu.CompilerParams(
            collective_id=0, has_side_effects=True, vmem_limit_bytes=60 * 1024 * 1024
        ),
        name="cg",
    )(
        residual, direction, legendre_scalar, legendre_plus, legendre_minus,
        jnp.transpose(noise_weight, (0, 2, 1, 3)), prior_inverse, order_ids.reshape(1, -1), cycle_assign.reshape(1, -1),
        order_ids, live_blocks, cycle_length, cycle_shift,
    )
    block = pl.BlockSpec((1, 1, sims, L), lambda i: (0, i, 0, 0))
    residual_next, direction_next, step = pl.pallas_call(
        functools.partial(update, sims),
        grid=(6,),
        out_shape=(
            jax.ShapeDtypeStruct(direction.shape, F32),
            jax.ShapeDtypeStruct(direction.shape, F32),
            jax.ShapeDtypeStruct((1, sims), F32),
        ),
        in_specs=[pl.BlockSpec((5 * sims, 128), lambda i: (0, 0)), block, block, block],
        out_specs=(block, block, pl.BlockSpec((1, sims), lambda i: (0, 0))),
        compiler_params=pltpu.CompilerParams(vmem_limit_bytes=60 * 1024 * 1024),
        name="update",
    )(stats, residual, direction, image)
    step_length = step.reshape(-1)
    return (residual_next, direction_next, step_length)


def solution(mesh):
    return jax.shard_map(
        functools.partial(body, nd=mesh.shape["dev"]),
        mesh=mesh,
        in_specs=(
            P("dev", None, None, None),
            P("dev", None, None, None),
            P("dev", None, None),
            P("dev", None, None),
            P("dev", None, None),
            P(),
            P("dev", None, None, None),
            P(),
            P("dev", None),
            P(),
            P("dev"),
            P("dev"),
        ),
        out_specs=(P("dev", None, None, None), P("dev", None, None, None), P()),
        check_vma=False,
    )
```

```python
import functools

import jax
import jax.numpy as jnp
from jax import lax
from jax.experimental import pallas as pl
from jax.experimental.pallas import tpu as pltpu
from jax.sharding import PartitionSpec as P

L = 3072
BLOCKS = 4
JC = 512
FC = 1024
PC = 512
F32 = jnp.float32
BF16 = jnp.bfloat16
NT = (((1,), (1,)), ((), ()))
MESH = pl.DeviceIdType.MESH


def dot(a, b):
    return jnp.dot(a, b, preferred_element_type=F32)


def dot_nt(a, b):
    return lax.dot_general(a, b, NT, preferred_element_type=F32)


def iota(shape, axis):
    return lax.broadcasted_iota(jnp.int32, shape, axis)


def turn(count, length):
    whole = 2 * length
    inv = 1.0 / whole.astype(F32)
    quot = jnp.floor(count.astype(F32) * inv).astype(jnp.int32)
    rest = count - quot * whole
    rest = jnp.where(rest < 0, rest + whole, rest)
    rest = jnp.where(rest >= whole, rest - whole, rest)
    t = (rest - length).astype(F32) * inv * F32(jnp.pi)
    t2 = t * t
    s = 1.0 / 6227020800.0
    for c in (-1.0 / 39916800, 1.0 / 362880, -1.0 / 5040, 1.0 / 120, -1.0 / 6, 1.0):
        s = s * t2 + c
    s = s * t
    k = 1.0 / 479001600.0
    for c in (-1.0 / 3628800, 1.0 / 40320, -1.0 / 720, 1.0 / 24, -0.5, 1.0):
        k = k * t2 + c
    return 2.0 * s * s - 1.0, -2.0 * s * k


def kernel(
    nd, slots, K, sims, pix,
    res_h, dir_h, ts_h, tp_h, tm_h, nw_h, prior_ref, ids_ref, assign_ref,
    ids_s, live_s, len_s, shift_s,
    image_h, stats_ref,
    res, drn, ts, teb, nw, E, acc_t, acc_eb, F, send1, recv1, send2, recv2,
    basis, weighted, PAR, lt, leb, prior, image, accs, psend, precv,
    in_sem, s1, r1, s2, r2, s3, r3, own_sem, out_sem,
):
    me = lax.axis_index("dev")
    groups = slots // 2
    half = 8 * nd
    total_rows = half * groups
    order_rows = 2 * nd
    cs = 3 * sims

    loads = [
        pltpu.make_async_copy(dir_h.at[0], drn, in_sem.at[0]),
        pltpu.make_async_copy(ts_h.at[0], ts, in_sem.at[1]),
        pltpu.make_async_copy(tp_h.at[0], teb.at[:, pl.ds(0, K)], in_sem.at[2]),
        pltpu.make_async_copy(tm_h.at[0], teb.at[:, pl.ds(K, K)], in_sem.at[3]),
        pltpu.make_async_copy(nw_h, nw, in_sem.at[4]),
        pltpu.make_async_copy(res_h.at[0], res, in_sem.at[5]),
    ]
    for load in loads:
        load.start()

    barrier = pltpu.get_barrier_semaphore()

    def greet(i, carry):
        pl.semaphore_signal(
            barrier, inc=1, device_id=(lax.rem(me + i, nd),), device_id_type=MESH
        )
        return carry

    lax.fori_loop(1, nd, greet, 0)

    my_m = ids_s[me]
    odd_sign = jnp.where(lax.rem(my_m, 2) == 0, F32(1.0), F32(-1.0))

    onehot_t = (iota((K, K), 0) == assign_ref[...]).astype(F32).astype(BF16)

    def build_e(c, carry):
        r0 = c * 128
        row = iota((128, K), 0) + r0
        cycle = (row // 8) % nd * slots + row // half * 2 + (row // 4) % 2
        pick = (cycle == iota((128, K), 1)).astype(F32).astype(BF16)
        block = dot_nt(pick, onehot_t)
        for oh in range(4):
            E[pl.ds(pl.multiple_of(r0, 128), 128), oh * K : (oh + 1) * K] = jnp.where(
                row % 4 == oh, block, 0.0
            ).astype(BF16)
        return carry

    lax.fori_loop(0, total_rows // 128, build_e, 0)

    for load in loads[:4]:
        load.wait()

    def lane_masks(j0, size=JC):
        lane = iota((1, size), 1) + j0
        return lane < L - my_m, lane % 2 == 0

    for c in range(L // FC):
        first, even = lane_masks(c * FC, FC)
        alt = jnp.where(even, 1.0, -1.0)
        m0 = first.astype(F32)
        m1 = 1.0 - m0
        x = drn[:, :, c * FC : (c + 1) * FC].reshape(6 * sims, FC)
        parts = [(x * m).astype(BF16) for m in (m0, m0 * alt, m1, m1 * alt)]
        lhs_t = jnp.concatenate([p[: 2 * sims] for p in parts], axis=0)
        lhs_eb = jnp.concatenate([p[2 * sims :] for p in parts], axis=0)
        add_t = dot(lhs_t, ts[c * FC : (c + 1) * FC, :])
        add_eb = dot(lhs_eb, teb[c * FC : (c + 1) * FC, :])
        if c == 0:
            acc_t[...] = add_t
            acc_eb[...] = add_eb
        else:
            acc_t[...] += add_t
            acc_eb[...] += add_eb

    def alive(s, height):
        return iota((height, K), 1) // (K // BLOCKS) < live_s[0, s]

    for s in range(2):
        g = F32(1.0) if s == 0 else odd_sign
        live = alive(s, sims)
        for h in range(2):
            a = 2 * s + h
            sg = F32(1.0) if h == 0 else g
            sx = F32(1.0) if h == 0 else -g
            t0 = 2 * sims * a
            e0 = 4 * sims * a
            t_re = sg * acc_t[t0 : t0 + sims, :]
            t_im = sg * acc_t[t0 + sims : t0 + 2 * sims, :]
            w = [sg * acc_eb[e0 + i * sims : e0 + (i + 1) * sims, 0:K] for i in range(4)]
            v = [sx * acc_eb[e0 + i * sims : e0 + (i + 1) * sims, K : 2 * K] for i in range(4)]
            zero = jnp.zeros((sims, K), F32)
            blocks = [
                t_re, v[3] - w[0], -(w[2] + v[1]), zero,
                t_im, -(w[1] + v[2]), v[0] - w[3], zero,
            ]
            for i, block in enumerate(blocks):
                F[i * sims : (i + 1) * sims, a * K : (a + 1) * K] = jnp.where(
                    live, block, 0.0
                ).astype(BF16)

    def pack(x):
        parts = [x[:, 0:128].reshape(nd, 8, 128), x[:, 128:256].reshape(nd, 8, 128)]
        return jnp.concatenate(parts, axis=1).astype(BF16)

    def unpack(x):
        x = x.astype(F32)
        parts = [x[:, 0:8].reshape(half, 128), x[:, 8:16].reshape(half, 128)]
        return jnp.concatenate(parts, axis=1)

    def remote(send, recv, ss, rs, g, i):
        dst = lax.rem(me + i, nd)
        return pltpu.make_async_remote_copy(
            src_ref=send if g is None else send.at[g, dst],
            dst_ref=recv.at[me] if g is None else recv.at[g, me],
            send_sem=ss.at[i] if g is None else ss.at[g, i],
            recv_sem=rs.at[i] if g is None else rs.at[g, i],
            device_id=(dst,),
            device_id_type=MESH,
        )

    def start_all(*args):
        def go(i, carry):
            remote(*args, i).start()
            return carry

        lax.fori_loop(1, nd, go, 0)

    def wait_recv_all(*args):
        def go(i, carry):
            remote(*args, i).wait_recv()
            return carry

        lax.fori_loop(1, nd, go, 0)

    def wait_send_all(*args):
        def go(i, carry):
            remote(*args, i).wait_send()
            return carry

        lax.fori_loop(1, nd, go, 0)

    def own(send, recv, e, g):
        return pltpu.make_async_copy(send.at[g, me], recv.at[g, me], own_sem.at[e, g])

    ex1 = (send1, recv1, s1, r1)
    ex2 = (send2, recv2, s2, r2)
    for g in range(groups):
        send1[g] = pack(dot_nt(E[g * half : (g + 1) * half, :], F[...]))
        if g == 0:
            pl.semaphore_wait(barrier, nd - 1)
        start_all(*ex1, g)
        own(send1, recv1, 0, g).start()

    ids = ids_ref[...].astype(F32)
    OB = min(64, order_rows)
    for ob in range(order_rows // OB):
        row = iota((OB, nd), 0) + ob * OB
        m_col = jnp.sum(
            jnp.where(iota((OB, nd), 1) == row // 2, ids, 0.0), axis=1, keepdims=True
        ).astype(jnp.int32)
        m_full = jnp.broadcast_to(m_col, (OB, 128))
        m_full = jnp.where(iota((OB, 128), 0) % 2 == 0, m_full, L - m_full)
        for tl in range(slots):
            n_full = jnp.full((OB, 128), len_s[tl], jnp.int32)
            spot = 2 * iota((OB, 128), 1) + shift_s[tl]
            co, si = turn(m_full * spot, n_full)
            wc, ws = turn(m_full * 256, n_full)

            def step(a, carry, tl=tl, ob=ob, wc=wc, ws=ws):
                re, im = carry
                at = pl.ds(pl.multiple_of(a * 128, 128), 128)
                basis[tl, ob * OB : (ob + 1) * OB, at] = re.astype(BF16)
                basis[tl, order_rows + ob * OB : order_rows + (ob + 1) * OB, at] = im.astype(BF16)
                return re * wc + im * ws, im * wc - re * ws

            lax.fori_loop(0, pix // 128, step, (2.0 * co, -2.0 * si))

    row = iota((2 * order_rows, nd), 0)
    odd = jnp.where(iota((2 * order_rows, nd), 1) == row % order_rows // 2, ids_ref[...] % 2, 0)
    odd = jnp.sum(odd.astype(F32), axis=1, keepdims=True)
    flips = (odd > 0.5) & (iota((2 * order_rows, 1), 0) % 2 == 1)
    g_col = jnp.where(flips, -1.0, 1.0)
    for h in range(2):
        weighted[h * 128 + cs : (h + 1) * 128, :] = jnp.zeros((128 - cs, pix), BF16)

    loads[4].wait()

    def slot(tl, D):
        mt = jnp.concatenate(
            [
                jnp.concatenate([D[0:order_rows, 0:128], D[order_rows:, 0:128]], axis=1),
                jnp.concatenate([D[0:order_rows, 128:256], D[order_rows:, 128:256]], axis=1),
            ],
            axis=0,
        )
        mm = mt.T
        M = jnp.concatenate([mm[0:cs], mm[128 : 128 + cs]], axis=0).astype(BF16)
        n = len_s[tl]
        for c in range(pix // PC):
            at = slice(c * PC, (c + 1) * PC)
            sky = dot(M, basis[tl, :, at]).reshape(2, 3, sims, PC)
            inside = iota((3, 2, PC), 2) + c * PC < n
            wt = jnp.where(inside, nw[tl, :, :, at], 0.0)
            for h in range(2):
                part = sky[h] * wt[:, h : h + 1, :]
                weighted[h * 128 : h * 128 + cs, at] = part.reshape(cs, PC).astype(BF16)
        back = dot_nt(basis[tl], weighted[...])
        north = back[:, 0:128]
        south = back[:, 128:256] * g_col
        for q, par in enumerate((north + south, north - south)):
            pt = par.astype(BF16)
            r0 = ((tl % 2) * 2 + q) * order_rows
            PAR[r0 : r0 + order_rows, 0:128] = pt[0:order_rows]
            PAR[r0 : r0 + order_rows, 128:256] = pt[order_rows:]

    a = iota((half, half), 0)
    want = (a // 2) % nd * 8 + a // (4 * nd) * 4 + a % 2 * 2 + a // (2 * nd) % 2
    gather = (iota((half, half), 1) == want).astype(F32).astype(BF16)
    want = ((a // 4 % 2 * 2 + a % 2) * nd + a // 8) * 2 + a // 2 % 2
    scatter = (iota((half, half), 1) == want).astype(F32).astype(BF16)
    for g in range(groups):
        own(send1, recv1, 0, g).wait()
        wait_recv_all(*ex1, g)
        D = dot(gather, unpack(recv1[g]).astype(BF16))
        for i in range(2):
            slot(2 * g + i, D[2 * i * order_rows : 2 * (i + 1) * order_rows])
        send2[g] = pack(dot(scatter, PAR[...]))
        start_all(*ex2, g)
        own(send2, recv2, 1, g).start()

    pr = prior_ref[...]
    sigma = jnp.maximum(jnp.max(jnp.abs(pr)), 1.0)
    pr8 = jnp.concatenate([pr, pr], axis=0)
    rolled = pltpu.roll(pr8, L - my_m, 1)
    first_row = iota((8, L), 1) < L - my_m
    prior[...] = jnp.where(first_row, rolled, pr8)
    inv_sigma = 1.0 / jnp.full((sims, 128), sigma, F32)

    loads[5].wait()

    def fold(x):
        x = x[0] + x[1] + x[2] + x[3] + x[4] + x[5]
        out = x[:, 0:128]
        for i in range(1, x.shape[1] // 128):
            out = out + x[:, i * 128 : (i + 1) * 128]
        return out

    norm = jnp.zeros((sims, 128), F32)
    for c in range(L // JC):
        x = res[:, :, c * JC : (c + 1) * JC]
        norm = norm + fold(x * x)
    accs[0:sims, :] = norm
    accs[sims : 4 * sims, :] = jnp.zeros((3 * sims, 128), F32)

    for g in range(groups):
        wait_send_all(*ex1, g)

    GT = None
    for g in range(groups):
        own(send2, recv2, 1, g).wait()
        wait_recv_all(*ex2, g)
        add = dot(unpack(recv2[g]).T.astype(BF16), E[g * half : (g + 1) * half, :])
        GT = add if GT is None else GT + add
    for s in range(2):
        live = alive(s, 256)
        G = [
            jnp.where(live, GT[:, (2 * s + q) * K : (2 * s + q + 1) * K], 0.0) for q in range(2)
        ]
        for q in range(2):
            a = 2 * s + q
            A, B = G[q], G[1 - q]
            lt[2 * sims * a : 2 * sims * a + sims, :] = A[0:sims].astype(BF16)
            lt[2 * sims * a + sims : 2 * sims * (a + 1), :] = A[128 : 128 + sims].astype(BF16)
            qr, ur = slice(sims, 2 * sims), slice(2 * sims, 3 * sims)
            qi, ui = slice(128 + sims, 128 + 2 * sims), slice(128 + 2 * sims, 128 + 3 * sims)
            plus = (-A[qr], -A[qi], -A[ur], -A[ui])
            minus = (B[ui], -B[ur], -B[qi], B[qr])
            for i in range(4):
                e0 = 4 * sims * a + i * sims
                leb[e0 : e0 + sims, 0:K] = plus[i].astype(BF16)
                leb[e0 : e0 + sims, K : 2 * K] = minus[i].astype(BF16)

    outs = []
    for c in range(L // JC):
        at = slice(c * JC, (c + 1) * JC)
        first, even = lane_masks(c * JC)
        nt = dot_nt(lt[...], ts[at, :])
        ne = dot_nt(leb[...], teb[at, :])

        def choose(x, size):
            x = [x[i * size : (i + 1) * size] for i in range(4)]
            return jnp.where(
                first, jnp.where(even, x[0], x[1]), jnp.where(even, x[2], x[3])
            )

        nt = choose(nt, 2 * sims).reshape(2, sims, JC)
        ne = choose(ne, 4 * sims).reshape(4, sims, JC)
        tt, te, ee, bb = [prior[i : i + 1, at][None] for i in range(4)]
        d = drn[:, :, at]
        img = jnp.concatenate(
            [
                nt + tt * d[0:2] + te * d[2:4],
                ne[0:2] + te * d[0:2] + ee * d[2:4],
                ne[2:4] + bb * d[4:6],
            ],
            axis=0,
        )
        image[:, :, at] = img
        out = pltpu.make_async_copy(image.at[:, :, at], image_h.at[0, :, :, at], out_sem.at[c])
        out.start()
        outs.append(out)
        scaled = img * inv_sigma[0:1, 0:1][None]
        accs[sims : 2 * sims, :] += fold(d * scaled)
        accs[2 * sims : 3 * sims, :] += fold(res[:, :, at] * scaled)
        accs[3 * sims : 4 * sims, :] += fold(scaled * scaled)

    local = jnp.sum(accs[...].T, axis=0, keepdims=True)
    psend[...] = jnp.broadcast_to(local, (8, 4 * sims))
    precv[me] = psend[...]
    ex3 = (psend, precv, s3, r3, None)
    start_all(*ex3)
    for out in outs:
        out.wait()
    for g in range(groups):
        wait_send_all(*ex2, g)
    wait_recv_all(*ex3)
    total = precv[0]
    for i in range(1, nd):
        total = total + precv[i]
    stats_ref[0 : 4 * sims, :] = jnp.broadcast_to(total.T[:, 0:1], (4 * sims, 128))
    stats_ref[4 * sims : 5 * sims, :] = jnp.full((sims, 128), sigma, F32)
    wait_send_all(*ex3)


def update(
    sims, stats, res_h, drn_h, img_h, res_out, dir_out, step_out, res, drn, img, in_sem, out_sem
):
    loads = []
    for c in range(6):
        triple = [(res_h, res), (drn_h, drn), (img_h, img)]
        for k, (src, dst) in enumerate(triple):
            load = pltpu.make_async_copy(src.at[0, c], dst.at[c], in_sem.at[k, c])
            load.start()
            loads.append(load)
    norm_old, da, ra, aa, sigma = [stats[i * sims : (i + 1) * sims, :] for i in range(5)]
    scaled = norm_old / da
    step = scaled / sigma
    ratio = (norm_old - 2.0 * scaled * ra + scaled * scaled * aa) / norm_old
    step_out[...] = step.T[0:1, :]
    stores = []
    for c in range(6):
        for load in loads[3 * c : 3 * c + 3]:
            load.wait()
        after = res[c] - step[:, 0:1] * img[c]
        res[c] = after
        drn[c] = after + ratio[:, 0:1] * drn[c]
        for k, (src, dst) in enumerate([(res, res_out), (drn, dir_out)]):
            store = pltpu.make_async_copy(src.at[c], dst.at[0, c], out_sem.at[k, c])
            store.start()
            stores.append(store)
    for store in stores:
        store.wait()


def body(
    residual, direction, legendre_scalar, legendre_plus, legendre_minus, prior_inverse,
    noise_weight, order_ids, live_blocks, cycle_assign, cycle_length, cycle_shift, nd,
):
    sims = direction.shape[2]
    K = legendre_scalar.shape[2]
    slots = cycle_length.shape[0]
    pix = noise_weight.shape[3]
    assert direction.shape[0] == 1
    assert slots % 2 == 0
    groups = slots // 2
    half = 8 * nd
    total_rows = half * groups
    vmem = pl.BlockSpec(memory_space=pltpu.VMEM)
    smem = pl.BlockSpec(memory_space=pltpu.SMEM)
    hbm = pl.BlockSpec(memory_space=pl.ANY)
    dma = pltpu.SemaphoreType.DMA
    image, stats = pl.pallas_call(
        functools.partial(kernel, nd, slots, K, sims, pix),
        out_shape=(
            jax.ShapeDtypeStruct(direction.shape, F32),
            jax.ShapeDtypeStruct((5 * sims, 128), F32),
        ),
        in_specs=[hbm] * 6 + [vmem] * 3 + [smem] * 4,
        out_specs=(hbm, vmem),
        scratch_shapes=[
            pltpu.VMEM((6, sims, L), F32),
            pltpu.VMEM((6, sims, L), F32),
            pltpu.VMEM((L, K), BF16),
            pltpu.VMEM((L, 2 * K), BF16),
            pltpu.VMEM((slots, 3, 2, pix), F32),
            pltpu.VMEM((total_rows, 4 * K), BF16),
            pltpu.VMEM((8 * sims, K), F32),
            pltpu.VMEM((16 * sims, 2 * K), F32),
            pltpu.VMEM((256, 4 * K), BF16),
            pltpu.VMEM((groups, nd, 16, 128), BF16),
            pltpu.VMEM((groups, nd, 16, 128), BF16),
            pltpu.VMEM((groups, nd, 16, 128), BF16),
            pltpu.VMEM((groups, nd, 16, 128), BF16),
            pltpu.VMEM((slots, 4 * nd, pix), BF16),
            pltpu.VMEM((256, pix), BF16),
            pltpu.VMEM((half, 256), BF16),
            pltpu.VMEM((8 * sims, K), BF16),
            pltpu.VMEM((16 * sims, 2 * K), BF16),
            pltpu.VMEM((8, L), F32),
            pltpu.VMEM((6, sims, L), F32),
            pltpu.VMEM((4 * sims, 128), F32),
            pltpu.VMEM((8, 4 * sims), F32),
            pltpu.VMEM((nd, 8, 4 * sims), F32),
            dma((6,)), *[dma((groups, nd))] * 4, dma((nd,)), dma((nd,)),
            dma((2, groups)), dma((L // JC,)),
        ],
        compiler_params=pltpu.CompilerParams(
            collective_id=0, has_side_effects=True, vmem_limit_bytes=60 * 1024 * 1024
        ),
        name="cg",
    )(
        residual, direction, legendre_scalar, legendre_plus, legendre_minus,
        jnp.transpose(noise_weight, (0, 2, 1, 3)), prior_inverse, order_ids.reshape(1, -1), cycle_assign.reshape(1, -1),
        order_ids, live_blocks, cycle_length, cycle_shift,
    )
    residual_next, direction_next, step = pl.pallas_call(
        functools.partial(update, sims),
        out_shape=(
            jax.ShapeDtypeStruct(direction.shape, F32),
            jax.ShapeDtypeStruct(direction.shape, F32),
            jax.ShapeDtypeStruct((1, sims), F32),
        ),
        in_specs=[vmem, hbm, hbm, hbm],
        out_specs=(hbm, hbm, vmem),
        scratch_shapes=[pltpu.VMEM((6, sims, L), F32)] * 3 + [dma((3, 6)), dma((2, 6))],
        compiler_params=pltpu.CompilerParams(vmem_limit_bytes=60 * 1024 * 1024),
        name="update",
    )(stats, residual, direction, image)
    step_length = step.reshape(-1)
    return (residual_next, direction_next, step_length)


def solution(mesh):
    return jax.shard_map(
        functools.partial(body, nd=mesh.shape["dev"]),
        mesh=mesh,
        in_specs=(
            P("dev", None, None, None),
            P("dev", None, None, None),
            P("dev", None, None),
            P("dev", None, None),
            P("dev", None, None),
            P(),
            P("dev", None, None, None),
            P(),
            P("dev", None),
            P(),
            P("dev"),
            P("dev"),
        ),
        out_specs=(P("dev", None, None, None), P("dev", None, None, None), P()),
        check_vma=False,
    )
```
